32 devices in a mesh: ctx: 8 (over z, x), head: 4 (over y, core).
Axes of the slice: x: 2, y: 2, z: 4, core: 2. Of those that a mesh axis runs over, the one named last changes fastest.
Arguments:
- query_states: bfloat16 [4096, 3584], P('ctx', 'head'), may hold values from -15 to 15
- key_states: bfloat16 [4096, 512], P('ctx', 'head'), may hold values from -6 to 6
- value_states: bfloat16 [4096, 512], P('ctx', 'head'), may hold values from -6 to 6
- out_weight: bfloat16 [3584, 3584], P('head'), may hold values from -0.29882812 to 0.29882812
- block_order: int32 [16], replicated, may hold values from 0 to 15, each once
- page_owner: int32 [256, 1], replicated, may hold values from 0 to 7; in each aligned block of 32 rows (0 to 31, 32 to 63, ...) at most 8 rows name the same one
- held_pages: int32 [8], replicated, may hold values from 0 to 64
Outputs:
- layer_output: bfloat16 [4096, 3584], P(('ctx', 'head'))
- page_values: bfloat16 [1024, 16, 1024], P('ctx', None, 'head')
- page_scales: float32 [8, 16384], P('head', 'ctx')
The draws below stay inside these ranges and needn't reach their ends.
Inputs may be any that keep to these rules, and one draw needn't show every extreme that they name: `block_order`: each number once. `page_owner`: among the pages of one device (aligned blocks of 32 rows) no owner is named more than 8 times.
All inputs are finite; a program needn't handle non-finite values. Where the reference program divides by a largest or mean magnitude, that divisor is 1e-20 or more.
Results may differ from the reference program's by a relative error of at most 0.012.
Values may be sent and summed in bfloat16 or wider, within the bound.
A program may use at most 64 MiB of HBM per device.

```python
import math
import jax
import jax.numpy as jnp
import numpy as np
from jax import lax

D = 3584
QH = 28
KVH = 4
HD = 128
PAGE = 16
BLOCK = 256
TOKENS = 4096
BLOCKS = 16
PAGES = 256
PAGES_DEV = 32
MOST = 8
SLOTS = 128
N_CTX = 8


def draw_query_states(key, part):
    key = jax.random.fold_in(key, 11)
    first_key = jax.random.fold_in(key, 0)
    result = jnp.clip(2.5 * jax.random.normal(first_key, (TOKENS, QH * HD), jnp.float32), -15.0, 15.0)
    return result.astype(jnp.bfloat16)


def draw_key_states(key, part):
    key = jax.random.fold_in(key, 17)
    first_key = jax.random.fold_in(key, 0)
    result = jnp.clip(jax.random.normal(first_key, (TOKENS, KVH * HD), jnp.float32), -6.0, 6.0)
    return result.astype(jnp.bfloat16)


def draw_held_pages(key, part):
    key = jax.random.fold_in(key, 23)
    first_key, second_key = jax.random.split(key)
    top_value = N_CTX * MOST
    drawn = jax.random.randint(first_key, (N_CTX,), 0, top_value + 1, jnp.int32)
    chosen = jax.random.randint(second_key, (), 0, N_CTX, jnp.int32)
    return jnp.where(jnp.arange(N_CTX, dtype=jnp.int32) == chosen, top_value, drawn).astype(jnp.int32)


def block_scale(stream_key, dims, pieces, least, high):
    def one(dim, shards_of):
        draws = jax.random.uniform(jax.random.fold_in(jax.random.fold_in(stream_key, 6), dim), (shards_of,), jnp.float32, least / len(pieces), high / len(pieces))
        return jnp.repeat(jnp.exp(draws), dims[dim] // shards_of).reshape((-1,) + (1,) * (len(dims) - dim - 1))

    loudness = one(*pieces[0])
    for cut in pieces[1:]:
        loudness = loudness * one(*cut)
    return loudness


def assign_block(stream_key, own, number, rows, count, top, bound, slope):
    sequence = jax.random.permutation(stream_key, count)
    heavy_load, common = portions_of(count, rows * top, bound, slope, True), portions_of(count, rows * top, bound, slope, False)
    places = jnp.arange(count)

    def named(sizes, turn):
        used = int((sizes > 0).sum())
        fixed = max(1, used // 4)
        passed = fixed + (places - fixed + turn * (used - fixed)) % max(1, count - fixed)
        return jnp.zeros((count,), jnp.int32).at[sequence[jnp.where(places < fixed, places, passed)]].set(jnp.asarray(sizes, jnp.int32))

    sizes = jnp.where(number % 4 == 0, named(heavy_load, number // 4), named(common, number - number // 4 - 1))
    mixed = jax.random.permutation(jax.random.fold_in(own, 3), count)
    donor, sink = mixed[0:count // 2 * 2:2], mixed[1:count // 2 * 2:2]
    slack = jnp.minimum(sizes[donor] - 1, bound - sizes[sink]) // 2
    slack = jnp.where((donor == sequence[0]) | (sink == sequence[0]) | (sizes[sink] == 0), 0, jnp.maximum(slack, 0))
    passed = jax.random.randint(jax.random.fold_in(own, 4), (count // 2,), 0, 1 << 20) % (slack + 1)
    sizes = sizes.at[donor].add(-passed).at[sink].add(passed)
    items = jnp.searchsorted(jnp.cumsum(sizes), jnp.arange(rows * top), side="right").astype(jnp.int32)
    listing = items.reshape(top, rows).T
    listing = listing[jax.random.permutation(jax.random.fold_in(own, 1), rows)]
    turn = jax.random.randint(jax.random.fold_in(own, 2), (rows, 1), 0, top)
    return jnp.take_along_axis(listing, (jnp.arange(top)[None, :] + turn) % top, axis=1)


def portions_of(number_of, total, reach, lean, full):
    loads = [(1 << 20) // math.isqrt(standing ** lean) + 1 for standing in range(1, number_of + 1)]
    largest = reach if full else min(reach, max(-(-total // number_of), total * loads[0] // sum(loads)))
    least = 1 if total - largest >= number_of - 1 else 0
    counts, rest = [largest] + [least] * (number_of - 1), total - largest - least * (number_of - 1)
    while rest > 0:
        movable = [i for i in range(1, number_of) if counts[i] < largest] or [i for i in range(1, number_of) if counts[i] < reach]
        mass, budget = sum([loads[i] for i in movable]), rest
        for i in movable:
            extra = min(reach - counts[i], max(1, budget * loads[i] // mass), rest)
            counts[i] = counts[i] + extra
            rest = rest - extra
    return np.array(counts)


def centred(key, extent, scale, bound, cuts=(), kind=jnp.bfloat16):
    level = block_scale(key, extent, cuts, -0.22, 0.18) if cuts else 1.0
    values = jax.random.normal(key, extent, jnp.float32) * scale * level
    return jnp.minimum(jnp.maximum(values, -bound), bound).astype(kind)


def setup_inputs(seed: int = 0) -> dict:
    arg_keys = jax.random.split(jax.random.key(seed), 8)
    query_states = draw_query_states(jax.random.fold_in(arg_keys[7], 71), 0)
    key_states = draw_key_states(jax.random.fold_in(arg_keys[7], 71), 0)
    value_states = centred(arg_keys[2], (TOKENS, KVH * HD), 1.0, 6.0, ((0, 8), (1, 4)))
    out_weight = centred(arg_keys[3], (QH * HD, D), 0.05, 0.29882812, ((0, 4),))
    block_order = jax.random.permutation(arg_keys[4], BLOCKS).astype(jnp.int32)
    page_owner_keys = jax.random.split(jax.random.fold_in(arg_keys[5], 1), PAGES // PAGES_DEV)
    page_owner_turns = jax.random.permutation(jax.random.fold_in(arg_keys[5], 3), PAGES // PAGES_DEV)
    page_owner = jax.vmap(lambda own, number: assign_block(jax.random.fold_in(arg_keys[5], 2), own, number, PAGES_DEV, N_CTX, 1, MOST, 2))(page_owner_keys, page_owner_turns).reshape((PAGES, 1))
    held_pages = draw_held_pages(jax.random.fold_in(arg_keys[7], 71), 0)
    return {"query_states": query_states, "key_states": key_states, "value_states": value_states, "out_weight": out_weight, "block_order": block_order, "page_owner": page_owner, "held_pages": held_pages}


def positions_of(block_order):
    offsets = jnp.arange(BLOCK, dtype=jnp.int32)
    return (block_order[:, None].astype(jnp.int32) * BLOCK + offsets[None, :]).reshape(-1).astype(jnp.int32)

def reference(query_states, key_states, value_states, out_weight, block_order, page_owner, held_pages):
    group_size = QH // KVH
    token_pos = positions_of(block_order)
    key_full = key_states.astype(jnp.float32).reshape(TOKENS, KVH, HD)
    value_full = value_states.astype(jnp.float32).reshape(TOKENS, KVH, HD)
    scaling = 1.0 / math.sqrt(HD)
    query_blocks = query_states.reshape(BLOCKS, BLOCK, QH * HD)
    pos_blocks = token_pos.reshape(BLOCKS, BLOCK)

    def one_block(block_pair):
        query_block, query_pos = block_pair
        query_heads = query_block.astype(jnp.float32).reshape(BLOCK, KVH, group_size, HD)
        scores = jnp.einsum('qhgd,khd->hgqk', query_heads, key_full) * scaling
        allowed = (token_pos[None, :] <= query_pos[:, None])[None, None]
        top_score = lax.optimization_barrier(jnp.max(jnp.where(allowed, scores, -1e+30), axis=-1))
        weights = jnp.where(allowed, jnp.exp(scores - top_score[..., None]), 0.0)
        norm_sum = lax.optimization_barrier(jnp.sum(weights, axis=-1))
        rounded = lax.optimization_barrier(weights.astype(jnp.bfloat16))
        weighted = jnp.einsum('hgqk,khd->qhgd', rounded.astype(jnp.float32), value_full)
        result = weighted / jnp.transpose(norm_sum, (2, 0, 1))[..., None]
        return result.reshape(BLOCK, QH * HD).astype(jnp.bfloat16)
    attended = lax.map(one_block, (query_blocks, pos_blocks)).reshape(TOKENS, QH * HD)
    layer_output = jnp.dot(attended, out_weight, preferred_element_type=jnp.float32).astype(jnp.bfloat16)
    owner_ids = page_owner[:, 0].astype(jnp.int32)
    owner_hot = (owner_ids[:, None] == jnp.arange(N_CTX, dtype=jnp.int32)[None, :]).astype(jnp.int32)
    page_rank = lax.optimization_barrier(jnp.sum((jnp.cumsum(owner_hot, axis=0) - 1) * owner_hot, axis=1)).astype(jnp.int32)
    slot_index = (held_pages.astype(jnp.int32)[owner_ids] + page_rank).astype(jnp.int32)
    store_row = (owner_ids * SLOTS + slot_index).astype(jnp.int32)
    kv_rows = jnp.stack([key_states.reshape(TOKENS, KVH, HD), value_states.reshape(TOKENS, KVH, HD)], axis=2)
    page_rows = kv_rows.reshape(PAGES, PAGE, KVH * 2 * HD)
    page_store = jnp.zeros((N_CTX * SLOTS, PAGE, KVH * 2 * HD), jnp.bfloat16).at[store_row].set(page_rows)
    split_store = page_store.astype(jnp.float32).reshape(N_CTX * SLOTS, PAGE, KVH * 2, HD)
    page_scale = lax.optimization_barrier(jnp.max(jnp.abs(split_store), axis=-1)) + 1e-06
    page_values = (split_store / page_scale[..., None]).astype(jnp.bfloat16).reshape(N_CTX * SLOTS, PAGE, KVH * 2 * HD)
    page_scales = jnp.transpose(page_scale.reshape(N_CTX * SLOTS * PAGE, KVH * 2))
    return (layer_output, page_values, page_scales)
```

```python
import functools
import math

import jax
import jax.numpy as jnp
from jax import lax
from jax.experimental import pallas as pl
from jax.experimental.pallas import tpu as pltpu
from jax.sharding import PartitionSpec as P

HD = 128
PAGE = 16
BLOCK = 256
BLOCK_PAGES = BLOCK // PAGE
COLS = 512
SUM_ROWS = 16
FAR = 1e30
EXP2_SCALE = math.log2(math.e) / math.sqrt(HD)
MESH = pl.DeviceIdType.MESH


def ring_place(index, n):
    odd = lax.rem(index, 2)
    half = lax.div(index, 2)
    return half * (1 - odd) + (n - 1 - half) * odd


def ring_index(place, n):
    place = lax.rem(place + 4 * n, n)
    back = lax.div(place, n // 2)
    return 2 * place * (1 - back) + (2 * (n - 1 - place) + 1) * back


def dot(a, b, dims):
    return lax.dot_general(a, b, (dims, ((), ())), preferred_element_type=jnp.float32)


def kernel(
    n, heads, q_hbm, k_hbm, v_hbm, w_hbm, order_ref, owner_ref, held_ref,
    out_hbm, values_hbm, scales_hbm,
    kv, q, w, top, acc, att, own, core_out, core_in, y_out, y_in, result,
    table, table_s, store, store_out, scale_out,
    in_sems, ring_send, ring_recv, core_send, core_recv, y_send, y_recv, table_sem, out_sems,
):
    me = lax.axis_index("ctx")
    head = lax.axis_index("head")
    core = lax.rem(head, 2)
    y = lax.div(head, 2)
    place = ring_place(me, n)
    right = ring_index(place + 1, n)
    left = ring_index(place - 1, n)
    core_peer = head + 1 - 2 * core
    y_peer = lax.rem(head + 2, 4)
    d_model = w.shape[1]
    steps = d_model // COLS
    half = BLOCK // 2

    own_pages = pl.ds(me * 2 * BLOCK_PAGES, 2 * BLOCK_PAGES)
    loads = [
        pltpu.make_async_copy(k_hbm, kv.at[own_pages, :, pl.ds(0, HD)], in_sems.at[0]),
        pltpu.make_async_copy(v_hbm, kv.at[own_pages, :, pl.ds(HD, HD)], in_sems.at[1]),
        pltpu.make_async_copy(q_hbm, q, in_sems.at[2]),
        pltpu.make_async_copy(w_hbm, w, in_sems.at[3]),
    ]
    for load in loads:
        load.start()

    barrier = pltpu.get_barrier_semaphore()
    for peer in ((left, head), (right, head), (me, core_peer), (me, y_peer)):
        pl.semaphore_signal(barrier, inc=1, device_id=peer, device_id_type=MESH)
    pl.semaphore_wait(barrier, 4)
    loads[0].wait()
    loads[1].wait()

    def block_of(lane, number):
        if lane == 0:
            return ring_index(place - lax.div(number, 2), n) * 2 + lax.rem(number, 2)
        return ring_index(place + lax.div(number, 2), n) * 2 + 1 - lax.rem(number, 2)

    def got_block(lane, number):
        if lane == 0:
            return ring_index(place - 1 - lax.div(number, 2), n) * 2 + lax.rem(number, 2)
        return ring_index(place + 1 + lax.div(number, 2), n) * 2 + 1 - lax.rem(number, 2)

    def block_rows(block):
        return pl.ds(pl.multiple_of(block * BLOCK, BLOCK), BLOCK)

    def keys_of(block):
        return kv[pl.ds(block * BLOCK_PAGES, BLOCK_PAGES), :, 0:HD].reshape(BLOCK, HD)

    def values_of(block):
        return kv[pl.ds(block * BLOCK_PAGES, BLOCK_PAGES), :, HD : 2 * HD].reshape(BLOCK, HD)

    def hop(lane, number, block):
        rows = pl.ds(block * BLOCK_PAGES, BLOCK_PAGES)
        return pltpu.make_async_remote_copy(
            src_ref=kv.at[rows],
            dst_ref=kv.at[rows],
            send_sem=ring_send.at[lane, number],
            recv_sem=ring_recv.at[lane, number],
            device_id=(right if lane == 0 else left, head),
            device_id_type=MESH,
        )

    for number in range(2):
        for lane in range(2):
            hop(lane, jnp.int32(number), block_of(lane, jnp.int32(number))).start()
    loads[2].wait()

    def penalty(key_block, query_block):
        return jnp.where(order_ref[key_block] < order_ref[query_block], 0.0, FAR)

    def with_sums(block_a, block_b):
        vals = jnp.concatenate(
            [values_of(block_a).T, values_of(block_b).T], axis=1
        )
        return jnp.concatenate([vals, jnp.ones((SUM_ROWS, 2 * BLOCK), jnp.bfloat16)], axis=0)

    def local_step(part):
        mine = me * 2 + part
        other = me * 2 + 1 - part
        pen = penalty(other, mine)
        key_a = keys_of(mine)
        key_b = keys_of(other)
        vals = with_sums(mine, other)
        causal = lax.broadcasted_iota(jnp.int32, (BLOCK, BLOCK), 0) <= lax.broadcasted_iota(
            jnp.int32, (BLOCK, BLOCK), 1
        )
        for g in range(heads):
            query = q[block_rows(part), g * HD : (g + 1) * HD]
            s_a = jnp.where(causal, dot(key_a, query, ((1,), (1,))), -FAR)
            s_b = dot(key_b, query, ((1,), (1,)))
            new_top = jnp.maximum(
                jnp.max(s_a, axis=0, keepdims=True), jnp.max(s_b, axis=0, keepdims=True) - pen
            )
            base = new_top * EXP2_SCALE
            p_a = jnp.exp2(s_a * EXP2_SCALE - base).astype(jnp.bfloat16)
            p_b = jnp.exp2(s_b * EXP2_SCALE - (base + pen)).astype(jnp.bfloat16)
            top[g : g + 1, :] = new_top
            acc[g] = dot(vals, jnp.concatenate([p_a, p_b], axis=0), ((1,), (0,)))

    def pair_step(part, number):
        mine = me * 2 + part
        block_a = got_block(0, number)
        block_b = got_block(1, number)
        pen_a = penalty(block_a, mine)
        pen_b = penalty(block_b, mine)
        key_a = keys_of(block_a)
        key_b = keys_of(block_b)
        vals = with_sums(block_a, block_b)
        for g in range(heads):
            query = q[block_rows(part), g * HD : (g + 1) * HD]
            s_a = dot(key_a, query, ((1,), (1,)))
            s_b = dot(key_b, query, ((1,), (1,)))
            old_top = top[g : g + 1, :]
            new_top = jnp.maximum(
                old_top,
                jnp.maximum(
                    jnp.max(s_a, axis=0, keepdims=True) - pen_a,
                    jnp.max(s_b, axis=0, keepdims=True) - pen_b,
                ),
            )
            base = new_top * EXP2_SCALE
            p_a = jnp.exp2(s_a * EXP2_SCALE - (base + pen_a)).astype(jnp.bfloat16)
            p_b = jnp.exp2(s_b * EXP2_SCALE - (base + pen_b)).astype(jnp.bfloat16)
            factor = jnp.exp2(old_top * EXP2_SCALE - base)
            top[g : g + 1, :] = new_top
            acc[g] = acc[g] * factor + dot(
                vals, jnp.concatenate([p_a, p_b], axis=0), ((1,), (0,))
            )

    def finish():
        for g in range(heads):
            done = acc[g]
            scaled = done[0:HD] * (1.0 / done[HD : HD + 1])
            att[:, g * HD : (g + 1) * HD] = scaled.T.astype(jnp.bfloat16)

    def core_copy(turn, step):
        cols = pl.ds(step * COLS, COLS)
        return pltpu.make_async_remote_copy(
            src_ref=core_out.at[turn, :, cols],
            dst_ref=core_in.at[turn, :, cols],
            send_sem=core_send.at[turn, step],
            recv_sem=core_recv.at[turn, step],
            device_id=(me, core_peer),
            device_id_type=MESH,
        )

    def y_copy(step):
        cols = pl.ds(step * COLS, COLS)
        return pltpu.make_async_remote_copy(
            src_ref=y_out.at[:, cols],
            dst_ref=y_in.at[:, cols],
            send_sem=y_send.at[step],
            recv_sem=y_recv.at[step],
            device_id=(me, y_peer),
            device_id_type=MESH,
        )

    def project(turn, use):
        rows = att[...]
        for step in range(steps + 1):
            if step < steps:
                cols = slice(step * COLS, (step + 1) * COLS)
                sums = dot(rows, w[:, cols], ((1,), (0,)))
                first, second = sums[0:half], sums[half:BLOCK]
                keep_first = core == 0
                own[:, cols] = jnp.where(keep_first, first, second)
                core_out[turn, :, cols] = jnp.where(keep_first, second, first).astype(jnp.bfloat16)
                core_copy(turn, step).start()
            if step > 0:
                last = step - 1
                cols = slice(last * COLS, (last + 1) * COLS)
                core_copy(turn, last).wait_recv()
                use(last, own[:, cols] + core_in[turn, :, cols].astype(jnp.float32), cols)

    local_step(1 - y)

    @pl.loop(0, n - 1)
    def _(number):
        for lane in range(2):
            hop(lane, number, got_block(lane, number)).wait_recv()

        @pl.when(number < n - 3)
        def _():
            for lane in range(2):
                hop(lane, number + 2, got_block(lane, number)).start()

        pair_step(1 - y, number)

    finish()
    loads[3].wait()

    def send_y(step, sums, cols):
        y_out[:, cols] = sums.astype(jnp.bfloat16)
        y_copy(step).start()

    project(0, send_y)

    local_step(y)

    @pl.loop(0, n - 1)
    def _(number):
        pair_step(y, number)

    finish()

    def hold(step, sums, cols):
        own[:, cols] = sums

    project(1, hold)

    pages = owner_ref.shape[0]
    slots = store.shape[0] // PAGE
    mine = (owner_ref[...] == me).astype(jnp.int32)
    page_row = lax.broadcasted_iota(jnp.int32, (pages, pages), 0)
    page_col = lax.broadcasted_iota(jnp.int32, (pages, pages), 1)
    mine_col = jnp.sum(jnp.where(page_row == page_col, mine, 0), axis=0, keepdims=True)
    rank_col = jnp.sum(jnp.where(page_row < page_col, mine, 0), axis=0, keepdims=True)
    slot_col = jnp.where(mine_col > 0, held_ref[me] + rank_col, -1)
    slot_row = jnp.broadcast_to(slot_col, (slots, pages)).T
    slot_number = lax.broadcasted_iota(jnp.int32, (pages, slots), 1)
    page_number = lax.broadcasted_iota(jnp.int32, (pages, slots), 0)
    table[...] = jnp.broadcast_to(
        jnp.sum(jnp.where(slot_row == slot_number, page_number + 1, 0), axis=0, keepdims=True),
        table.shape,
    )
    to_scalars = pltpu.make_async_copy(table, table_s, table_sem)
    to_scalars.start()
    to_scalars.wait()

    @pl.loop(0, slots)
    def _(slot):
        entry = table_s[0, slot]
        held = jnp.where(entry > 0, 1.0, 0.0)
        page = kv[jnp.maximum(entry - 1, 0)].astype(jnp.float32) * held
        store[pl.ds(pl.multiple_of(slot * PAGE, PAGE), PAGE), :] = page

    @pl.loop(0, slots * PAGE // HD)
    def _(group):
        rows = pl.ds(pl.multiple_of(group * HD, HD), HD)
        for t in range(2):
            entries = store[rows, t * HD : (t + 1) * HD]
            size = jnp.abs(entries)
            scale = jnp.max(size, axis=1, keepdims=True) + 1e-06
            store_out[rows, t * HD : (t + 1) * HD] = (entries / scale).astype(jnp.bfloat16)
            scale_out[t : t + 1, rows] = jnp.max(size.T, axis=0, keepdims=True) + 1e-06

    page_copies = [
        pltpu.make_async_copy(store_out, values_hbm, out_sems.at[0]),
        pltpu.make_async_copy(scale_out, scales_hbm, out_sems.at[1]),
    ]
    for copy in page_copies:
        copy.start()

    out_copies = []
    for step in range(steps):
        cols = slice(step * COLS, (step + 1) * COLS)
        y_copy(step).wait_recv()
        result[:, cols] = (own[:, cols] + y_in[:, cols].astype(jnp.float32)).astype(jnp.bfloat16)
        span = pl.ds(step * COLS, COLS)
        copy = pltpu.make_async_copy(result.at[:, span], out_hbm.at[:, span], out_sems.at[2 + step])
        copy.start()
        out_copies.append(copy)

    @pl.loop(0, n - 1)
    def _(number):
        for lane in range(2):
            hop(lane, number, block_of(lane, number)).wait_send()

    for step in range(steps):
        core_copy(0, step).wait_send()
        core_copy(1, step).wait_send()
        y_copy(step).wait_send()
    for copy in page_copies + out_copies:
        copy.wait()


def shards(query_states, key_states, value_states, out_weight, block_order, page_owner, held_pages):
    n = lax.axis_size("ctx")
    tok_rows, col_count = query_states.shape
    d_model = out_weight.shape[1]
    heads = col_count // HD
    tokens = n * tok_rows
    pages_dev = tok_rows // PAGE
    slots = 2 * n * max(2, 2 * pages_dev // n)
    steps = d_model // COLS
    part = tok_rows // 4
    bf16, f32 = jnp.bfloat16, jnp.float32
    any_space = pl.BlockSpec(memory_space=pl.ANY)
    smem = pl.BlockSpec(memory_space=pltpu.SMEM)
    vmem = pl.BlockSpec(memory_space=pltpu.VMEM)
    layer_output, values, scales = pl.pallas_call(
        functools.partial(kernel, n, heads),
        out_shape=(
            jax.ShapeDtypeStruct((part, d_model), bf16),
            jax.ShapeDtypeStruct((slots * PAGE, 2 * HD), bf16),
            jax.ShapeDtypeStruct((2, slots * PAGE), f32),
        ),
        in_specs=[any_space] * 4 + [smem, vmem, smem],
        out_specs=(any_space,) * 3,
        scratch_shapes=[
            pltpu.VMEM((tokens // PAGE, PAGE, 2 * HD), bf16),
            pltpu.VMEM((tok_rows, col_count), bf16),
            pltpu.VMEM(out_weight.shape, bf16),
            pltpu.VMEM((8, BLOCK), f32),
            pltpu.VMEM((heads, HD + SUM_ROWS, BLOCK), f32),
            pltpu.VMEM((BLOCK, col_count), bf16),
            pltpu.VMEM((part, d_model), f32),
            pltpu.VMEM((2, part, d_model), bf16),
            pltpu.VMEM((2, part, d_model), bf16),
            pltpu.VMEM((part, d_model), bf16),
            pltpu.VMEM((part, d_model), bf16),
            pltpu.VMEM((part, d_model), bf16),
            pltpu.VMEM((8, slots), jnp.int32),
            pltpu.SMEM((8, slots), jnp.int32),
            pltpu.VMEM((slots * PAGE, 2 * HD), f32),
            pltpu.VMEM((slots * PAGE, 2 * HD), bf16),
            pltpu.VMEM((2, slots * PAGE), f32),
            pltpu.SemaphoreType.DMA((4,)),
            pltpu.SemaphoreType.DMA((2, n - 1)),
            pltpu.SemaphoreType.DMA((2, n - 1)),
            pltpu.SemaphoreType.DMA((2, steps)),
            pltpu.SemaphoreType.DMA((2, steps)),
            pltpu.SemaphoreType.DMA((steps,)),
            pltpu.SemaphoreType.DMA((steps,)),
            pltpu.SemaphoreType.DMA,
            pltpu.SemaphoreType.DMA((2 + steps,)),
        ],
        compiler_params=pltpu.CompilerParams(
            collective_id=0, has_side_effects=True, vmem_limit_bytes=48 * 1024 * 1024
        ),
    )(
        query_states,
        key_states.reshape(-1, PAGE, HD),
        value_states.reshape(-1, PAGE, HD),
        out_weight,
        block_order,
        page_owner,
        held_pages,
    )
    return layer_output, values.reshape(slots, PAGE, 2 * HD), scales


def solution(mesh):
    in_specs = (
        P("ctx", "head"),
        P("ctx", "head"),
        P("ctx", "head"),
        P("head", None),
        P(),
        P(),
        P(),
    )
    out_specs = (P(("ctx", "head"), None), P("ctx", None, "head"), P("head", "ctx"))
    return jax.shard_map(shards, mesh=mesh, in_specs=in_specs, out_specs=out_specs, check_vma=False)
```

```python
import functools
import math

import jax
import jax.numpy as jnp
from jax import lax
from jax.experimental import pallas as pl
from jax.experimental.pallas import tpu as pltpu
from jax.sharding import PartitionSpec as P

HD = 128
PAGE = 16
BLOCK = 256
BLOCK_PAGES = BLOCK // PAGE
COLS = 512
SUM_ROWS = 16
FAR = 1e30
EXP2_SCALE = math.log2(math.e) / math.sqrt(HD)
MESH = pl.DeviceIdType.MESH


def ring_place(index, n):
    odd = lax.rem(index, 2)
    half = lax.div(index, 2)
    return half * (1 - odd) + (n - 1 - half) * odd


def ring_index(place, n):
    place = lax.rem(place + 4 * n, n)
    back = lax.div(place, n // 2)
    return 2 * place * (1 - back) + (2 * (n - 1 - place) + 1) * back


def dot(a, b, dims):
    return lax.dot_general(a, b, (dims, ((), ())), preferred_element_type=jnp.float32)


def kernel(
    n, heads, q_hbm, k_hbm, v_hbm, w_hbm, order_ref, owner_ref, held_ref,
    out_hbm, values_hbm, scales_hbm,
    kv, q, q_t, w, top, acc, att, own, core_out, core_in, y_out, y_in, result,
    table, table_s, store, store_out, scale_out,
    in_sems, ring_send, ring_recv, core_send, core_recv, y_send, y_recv, table_sem, out_sems,
):
    me = lax.axis_index("ctx")
    head = lax.axis_index("head")
    core = lax.rem(head, 2)
    y = lax.div(head, 2)
    place = ring_place(me, n)
    right = ring_index(place + 1, n)
    left = ring_index(place - 1, n)
    core_peer = head + 1 - 2 * core
    y_peer = lax.rem(head + 2, 4)
    d_model = w.shape[1]
    steps = d_model // COLS
    half = BLOCK // 2

    own_pages = pl.ds(me * 2 * BLOCK_PAGES, 2 * BLOCK_PAGES)
    loads = [
        pltpu.make_async_copy(k_hbm, kv.at[own_pages, :, pl.ds(0, HD)], in_sems.at[0]),
        pltpu.make_async_copy(v_hbm, kv.at[own_pages, :, pl.ds(HD, HD)], in_sems.at[1]),
        pltpu.make_async_copy(q_hbm, q, in_sems.at[2]),
        pltpu.make_async_copy(w_hbm, w, in_sems.at[3]),
    ]
    for load in loads:
        load.start()

    barrier = pltpu.get_barrier_semaphore()
    for peer in ((left, head), (right, head), (me, core_peer), (me, y_peer)):
        pl.semaphore_signal(barrier, inc=1, device_id=peer, device_id_type=MESH)
    pl.semaphore_wait(barrier, 4)
    loads[0].wait()
    loads[1].wait()

    def block_of(lane, number):
        if lane == 0:
            return ring_index(place - lax.div(number, 2), n) * 2 + lax.rem(number, 2)
        return ring_index(place + lax.div(number, 2), n) * 2 + 1 - lax.rem(number, 2)

    def got_block(lane, number):
        if lane == 0:
            return ring_index(place - 1 - lax.div(number, 2), n) * 2 + lax.rem(number, 2)
        return ring_index(place + 1 + lax.div(number, 2), n) * 2 + 1 - lax.rem(number, 2)

    def block_rows(block):
        return pl.ds(pl.multiple_of(block * BLOCK, BLOCK), BLOCK)

    def keys_of(block):
        return kv[pl.ds(block * BLOCK_PAGES, BLOCK_PAGES), :, 0:HD].reshape(BLOCK, HD)

    def values_of(block):
        return kv[pl.ds(block * BLOCK_PAGES, BLOCK_PAGES), :, HD : 2 * HD].reshape(BLOCK, HD)

    def hop(lane, number, block):
        rows = pl.ds(block * BLOCK_PAGES, BLOCK_PAGES)
        return pltpu.make_async_remote_copy(
            src_ref=kv.at[rows],
            dst_ref=kv.at[rows],
            send_sem=ring_send.at[lane, number],
            recv_sem=ring_recv.at[lane, number],
            device_id=(right if lane == 0 else left, head),
            device_id_type=MESH,
        )

    for number in range(2):
        for lane in range(2):
            hop(lane, jnp.int32(number), block_of(lane, jnp.int32(number))).start()
    loads[2].wait()
    for g in range(heads):
        for part in range(2):
            rows = slice(part * BLOCK, (part + 1) * BLOCK)
            q_t[part, g] = q[rows, g * HD : (g + 1) * HD].T

    def penalty(key_block, query_block):
        return jnp.where(order_ref[key_block] < order_ref[query_block], 0.0, FAR)

    def with_sums(block_a, block_b):
        vals = jnp.concatenate(
            [values_of(block_a).T, values_of(block_b).T], axis=1
        )
        return jnp.concatenate([vals, jnp.ones((SUM_ROWS, 2 * BLOCK), jnp.bfloat16)], axis=0)

    def local_step(slot, part):
        mine = me * 2 + part
        other = me * 2 + 1 - part
        pen = penalty(other, mine)
        key_a = keys_of(mine)
        key_b = keys_of(other)
        vals = with_sums(mine, other)
        causal = lax.broadcasted_iota(jnp.int32, (BLOCK, BLOCK), 0) <= lax.broadcasted_iota(
            jnp.int32, (BLOCK, BLOCK), 1
        )
        for g in range(heads):
            query = q_t[part, g]
            s_a = jnp.where(causal, dot(key_a, query, ((1,), (0,))), -FAR)
            s_b = dot(key_b, query, ((1,), (0,)))
            new_top = jnp.maximum(
                jnp.max(s_a, axis=0, keepdims=True), jnp.max(s_b, axis=0, keepdims=True) - pen
            )
            base = new_top * EXP2_SCALE
            p_a = jnp.exp2(s_a * EXP2_SCALE - base).astype(jnp.bfloat16)
            p_b = jnp.exp2(s_b * EXP2_SCALE - (base + pen)).astype(jnp.bfloat16)
            top[slot, g : g + 1, :] = new_top
            acc[slot, g] = dot(vals, jnp.concatenate([p_a, p_b], axis=0), ((1,), (0,)))

    def pair_step(slot, part, number):
        mine = me * 2 + part
        block_a = got_block(0, number)
        block_b = got_block(1, number)
        pen_a = penalty(block_a, mine)
        pen_b = penalty(block_b, mine)
        key_a = keys_of(block_a)
        key_b = keys_of(block_b)
        vals = with_sums(block_a, block_b)
        for g in range(heads):
            query = q_t[part, g]
            s_a = dot(key_a, query, ((1,), (0,)))
            s_b = dot(key_b, query, ((1,), (0,)))
            old_top = top[slot, g : g + 1, :]
            new_top = jnp.maximum(
                old_top,
                jnp.maximum(
                    jnp.max(s_a, axis=0, keepdims=True) - pen_a,
                    jnp.max(s_b, axis=0, keepdims=True) - pen_b,
                ),
            )
            base = new_top * EXP2_SCALE
            p_a = jnp.exp2(s_a * EXP2_SCALE - (base + pen_a)).astype(jnp.bfloat16)
            p_b = jnp.exp2(s_b * EXP2_SCALE - (base + pen_b)).astype(jnp.bfloat16)
            factor = jnp.exp2(old_top * EXP2_SCALE - base)
            top[slot, g : g + 1, :] = new_top
            acc[slot, g] = acc[slot, g] * factor + dot(
                vals, jnp.concatenate([p_a, p_b], axis=0), ((1,), (0,))
            )

    def finish(slot):
        for g in range(heads):
            done = acc[slot, g]
            scaled = done[0:HD] * (1.0 / done[HD : HD + 1])
            att[:, g * HD : (g + 1) * HD] = scaled.T.astype(jnp.bfloat16)

    def core_copy(turn, step):
        cols = pl.ds(step * COLS, COLS)
        return pltpu.make_async_remote_copy(
            src_ref=core_out.at[turn, :, cols],
            dst_ref=core_in.at[turn, :, cols],
            send_sem=core_send.at[turn, step],
            recv_sem=core_recv.at[turn, step],
            device_id=(me, core_peer),
            device_id_type=MESH,
        )

    def y_copy(step):
        cols = pl.ds(step * COLS, COLS)
        return pltpu.make_async_remote_copy(
            src_ref=y_out.at[:, cols],
            dst_ref=y_in.at[:, cols],
            send_sem=y_send.at[step],
            recv_sem=y_recv.at[step],
            device_id=(me, y_peer),
            device_id_type=MESH,
        )

    def project(turn):
        rows = att[...]
        for step in range(steps):
            cols = slice(step * COLS, (step + 1) * COLS)
            sums = dot(rows, w[:, cols], ((1,), (0,)))
            first, second = sums[0:half], sums[half:BLOCK]
            keep_first = core == 0
            own[:, cols] = jnp.where(keep_first, first, second)
            core_out[turn, :, cols] = jnp.where(keep_first, second, first).astype(jnp.bfloat16)
            core_copy(turn, step).start()

    def both_cores(turn, step):
        cols = slice(step * COLS, (step + 1) * COLS)
        core_copy(turn, step).wait_recv()
        return own[:, cols] + core_in[turn, :, cols].astype(jnp.float32), cols

    local_step(0, 1 - y)
    local_step(1, y)

    @pl.loop(0, n - 1)
    def _(number):
        for lane in range(2):
            hop(lane, number, got_block(lane, number)).wait_recv()

        @pl.when(number < n - 3)
        def _():
            for lane in range(2):
                hop(lane, number + 2, got_block(lane, number)).start()

        pair_step(0, 1 - y, number)

    finish(0)
    loads[3].wait()

    project(0)
    for step in range(steps):
        sums, cols = both_cores(0, step)
        y_out[:, cols] = sums.astype(jnp.bfloat16)
        y_copy(step).start()

    @pl.loop(0, n - 1)
    def _(number):
        pair_step(1, y, number)

    finish(1)

    project(1)

    pages = owner_ref.shape[1]
    slots = store.shape[0] // PAGE
    mine_col = (owner_ref[...] == me).astype(jnp.int32)
    mine = jnp.broadcast_to(mine_col, (slots, pages)).T[:, 0:1]
    page_row = lax.broadcasted_iota(jnp.int32, (pages, pages), 0)
    page_col = lax.broadcasted_iota(jnp.int32, (pages, pages), 1)
    rank_col = jnp.sum(jnp.where(page_row < page_col, mine, 0), axis=0, keepdims=True)
    slot_col = jnp.where(mine_col > 0, held_ref[me] + rank_col, -1)
    slot_row = jnp.broadcast_to(slot_col, (slots, pages)).T
    slot_number = lax.broadcasted_iota(jnp.int32, (pages, slots), 1)
    page_number = lax.broadcasted_iota(jnp.int32, (pages, slots), 0)
    table[...] = jnp.broadcast_to(
        jnp.sum(jnp.where(slot_row == slot_number, page_number + 1, 0), axis=0, keepdims=True),
        table.shape,
    )
    to_scalars = pltpu.make_async_copy(table, table_s, table_sem)
    to_scalars.start()
    to_scalars.wait()

    @pl.loop(0, slots, unroll=8)
    def _(slot):
        entry = table_s[0, slot]
        held = jnp.where(entry > 0, 1.0, 0.0)
        page = kv[jnp.maximum(entry - 1, 0)].astype(jnp.float32) * held
        store[pl.ds(pl.multiple_of(slot * PAGE, PAGE), PAGE), :] = page

    @pl.loop(0, slots * PAGE // HD, unroll=2)
    def _(group):
        rows = pl.ds(pl.multiple_of(group * HD, HD), HD)
        for t in range(2):
            entries = store[rows, t * HD : (t + 1) * HD]
            size = jnp.abs(entries)
            scale = jnp.max(size, axis=1, keepdims=True) + 1e-06
            store_out[rows, t * HD : (t + 1) * HD] = (entries / scale).astype(jnp.bfloat16)
            scale_out[t : t + 1, rows] = jnp.max(size.T, axis=0, keepdims=True) + 1e-06

    page_copies = [
        pltpu.make_async_copy(store_out, values_hbm, out_sems.at[0]),
        pltpu.make_async_copy(scale_out, scales_hbm, out_sems.at[1]),
    ]
    for copy in page_copies:
        copy.start()

    out_copies = []
    for step in range(steps):
        sums, cols = both_cores(1, step)
        y_copy(step).wait_recv()
        result[:, cols] = (sums + y_in[:, cols].astype(jnp.float32)).astype(jnp.bfloat16)
        span = pl.ds(step * COLS, COLS)
        copy = pltpu.make_async_copy(result.at[:, span], out_hbm.at[:, span], out_sems.at[2 + step])
        copy.start()
        out_copies.append(copy)

    @pl.loop(0, n - 1)
    def _(number):
        for lane in range(2):
            hop(lane, number, block_of(lane, number)).wait_send()

    for step in range(steps):
        core_copy(0, step).wait_send()
        core_copy(1, step).wait_send()
        y_copy(step).wait_send()
    for copy in page_copies + out_copies:
        copy.wait()


def shards(query_states, key_states, value_states, out_weight, block_order, page_owner, held_pages):
    n = lax.axis_size("ctx")
    tok_rows, col_count = query_states.shape
    d_model = out_weight.shape[1]
    heads = col_count // HD
    tokens = n * tok_rows
    pages_dev = tok_rows // PAGE
    slots = 2 * n * max(2, 2 * pages_dev // n)
    steps = d_model // COLS
    part = tok_rows // 4
    bf16, f32 = jnp.bfloat16, jnp.float32
    hbm = pl.BlockSpec(memory_space=pltpu.HBM)
    smem = pl.BlockSpec(memory_space=pltpu.SMEM)
    vmem = pl.BlockSpec(memory_space=pltpu.VMEM)
    layer_output, values, scales = pl.pallas_call(
        functools.partial(kernel, n, heads),
        out_shape=(
            jax.ShapeDtypeStruct((part, d_model), bf16),
            jax.ShapeDtypeStruct((slots * PAGE, 2 * HD), bf16),
            jax.ShapeDtypeStruct((2, slots * PAGE), f32),
        ),
        in_specs=[hbm] * 4 + [smem, vmem, smem],
        out_specs=(hbm,) * 3,
        scratch_shapes=[
            pltpu.VMEM((tokens // PAGE, PAGE, 2 * HD), bf16),
            pltpu.VMEM((tok_rows, col_count), bf16),
            pltpu.VMEM((2, heads, HD, BLOCK), bf16),
            pltpu.VMEM(out_weight.shape, bf16),
            pltpu.VMEM((2, 8, BLOCK), f32),
            pltpu.VMEM((2, heads, HD + SUM_ROWS, BLOCK), f32),
            pltpu.VMEM((BLOCK, col_count), bf16),
            pltpu.VMEM((part, d_model), f32),
            pltpu.VMEM((2, part, d_model), bf16),
            pltpu.VMEM((2, part, d_model), bf16),
            pltpu.VMEM((part, d_model), bf16),
            pltpu.VMEM((part, d_model), bf16),
            pltpu.VMEM((part, d_model), bf16),
            pltpu.VMEM((8, slots), jnp.int32),
            pltpu.SMEM((8, slots), jnp.int32),
            pltpu.VMEM((slots * PAGE, 2 * HD), f32),
            pltpu.VMEM((slots * PAGE, 2 * HD), bf16),
            pltpu.VMEM((2, slots * PAGE), f32),
            pltpu.SemaphoreType.DMA((4,)),
            pltpu.SemaphoreType.DMA((2, n - 1)),
            pltpu.SemaphoreType.DMA((2, n - 1)),
            pltpu.SemaphoreType.DMA((2, steps)),
            pltpu.SemaphoreType.DMA((2, steps)),
            pltpu.SemaphoreType.DMA((steps,)),
            pltpu.SemaphoreType.DMA((steps,)),
            pltpu.SemaphoreType.DMA,
            pltpu.SemaphoreType.DMA((2 + steps,)),
        ],
        compiler_params=pltpu.CompilerParams(
            collective_id=0, has_side_effects=True, vmem_limit_bytes=63 * 1024 * 1024
        ),
    )(
        query_states,
        key_states.reshape(-1, PAGE, HD),
        value_states.reshape(-1, PAGE, HD),
        out_weight,
        block_order,
        page_owner.reshape(1, -1),
        held_pages,
    )
    return layer_output, values.reshape(slots, PAGE, 2 * HD), scales


def solution(mesh):
    in_specs = (
        P("ctx", "head"),
        P("ctx", "head"),
        P("ctx", "head"),
        P("head", None),
        P(),
        P(),
        P(),
    )
    out_specs = (P(("ctx", "head"), None), P("ctx", None, "head"), P("head", "ctx"))
    return jax.shard_map(shards, mesh=mesh, in_specs=in_specs, out_specs=out_specs, check_vma=False)
```

```python
import functools
import math

import jax
import jax.numpy as jnp
from jax import lax
from jax.experimental import pallas as pl
from jax.experimental.pallas import tpu as pltpu
from jax.sharding import PartitionSpec as P

HD = 128
PAGE = 16
BLOCK = 256
BLOCK_PAGES = BLOCK // PAGE
COLS = 512
SUM_ROWS = 16
FAR = 1e30
EXP2_SCALE = math.log2(math.e) / math.sqrt(HD)
MESH = pl.DeviceIdType.MESH


def ring_place(index, n):
    odd = lax.rem(index, 2)
    half = lax.div(index, 2)
    return half * (1 - odd) + (n - 1 - half) * odd


def ring_index(place, n):
    place = lax.rem(place + 4 * n, n)
    back = lax.div(place, n // 2)
    return 2 * place * (1 - back) + (2 * (n - 1 - place) + 1) * back


def dot(a, b, dims):
    return lax.dot_general(a, b, (dims, ((), ())), preferred_element_type=jnp.float32)


def kernel(
    n, heads, q_hbm, k_hbm, v_hbm, w_hbm, order_ref, owner_ref, held_ref,
    out_hbm, values_hbm, scales_hbm,
    kv, q, q_t, w, top, acc, att, own, core_out, core_in, y_out, y_in, result,
    table, table_s, store_out, scale_out,
    in_sems, ring_send, ring_recv, core_send, core_recv, y_send, y_recv, table_sem, out_sems,
):
    me = lax.axis_index("ctx")
    head = lax.axis_index("head")
    core = lax.rem(head, 2)
    y = lax.div(head, 2)
    place = ring_place(me, n)
    right = ring_index(place + 1, n)
    left = ring_index(place - 1, n)
    core_peer = head + 1 - 2 * core
    y_peer = lax.rem(head + 2, 4)
    d_model = w.shape[1]
    steps = d_model // COLS
    half = BLOCK // 2

    own_pages = pl.ds(me * 2 * BLOCK_PAGES, 2 * BLOCK_PAGES)
    loads = [
        pltpu.make_async_copy(k_hbm, kv.at[own_pages, :, pl.ds(0, HD)], in_sems.at[0]),
        pltpu.make_async_copy(v_hbm, kv.at[own_pages, :, pl.ds(HD, HD)], in_sems.at[1]),
        pltpu.make_async_copy(q_hbm, q, in_sems.at[2]),
        pltpu.make_async_copy(w_hbm, w, in_sems.at[3]),
    ]
    for load in loads:
        load.start()

    barrier = pltpu.get_barrier_semaphore()
    for peer in ((left, head), (right, head), (me, core_peer), (me, y_peer)):
        pl.semaphore_signal(barrier, inc=1, device_id=peer, device_id_type=MESH)
    pl.semaphore_wait(barrier, 4)
    loads[0].wait()
    loads[1].wait()

    def block_of(lane, number):
        if lane == 0:
            return ring_index(place - lax.div(number, 2), n) * 2 + lax.rem(number, 2)
        return ring_index(place + lax.div(number, 2), n) * 2 + 1 - lax.rem(number, 2)

    def got_block(lane, number):
        if lane == 0:
            return ring_index(place - 1 - lax.div(number, 2), n) * 2 + lax.rem(number, 2)
        return ring_index(place + 1 + lax.div(number, 2), n) * 2 + 1 - lax.rem(number, 2)

    def block_rows(block):
        return pl.ds(pl.multiple_of(block * BLOCK, BLOCK), BLOCK)

    def keys_of(block):
        return kv[pl.ds(block * BLOCK_PAGES, BLOCK_PAGES), :, 0:HD].reshape(BLOCK, HD)

    def values_of(block):
        return kv[pl.ds(block * BLOCK_PAGES, BLOCK_PAGES), :, HD : 2 * HD].reshape(BLOCK, HD)

    def hop(lane, number, block):
        rows = pl.ds(block * BLOCK_PAGES, BLOCK_PAGES)
        return pltpu.make_async_remote_copy(
            src_ref=kv.at[rows],
            dst_ref=kv.at[rows],
            send_sem=ring_send.at[lane, number],
            recv_sem=ring_recv.at[lane, number],
            device_id=(right if lane == 0 else left, head),
            device_id_type=MESH,
        )

    for number in range(2):
        for lane in range(2):
            hop(lane, jnp.int32(number), block_of(lane, jnp.int32(number))).start()
    loads[2].wait()
    for g in range(heads):
        for part in range(2):
            rows = slice(part * BLOCK, (part + 1) * BLOCK)
            q_t[part, g] = q[rows, g * HD : (g + 1) * HD].T

    def penalty(key_block, query_block):
        return jnp.where(order_ref[key_block] < order_ref[query_block], 0.0, FAR)

    def with_sums(block_a, block_b):
        vals = jnp.concatenate(
            [values_of(block_a).T, values_of(block_b).T], axis=1
        )
        return jnp.concatenate([vals, jnp.ones((SUM_ROWS, 2 * BLOCK), jnp.bfloat16)], axis=0)

    def local_step(slot, part):
        mine = me * 2 + part
        other = me * 2 + 1 - part
        pen = penalty(other, mine)
        key_a = keys_of(mine)
        key_b = keys_of(other)
        vals = with_sums(mine, other)
        causal = lax.broadcasted_iota(jnp.int32, (BLOCK, BLOCK), 0) <= lax.broadcasted_iota(
            jnp.int32, (BLOCK, BLOCK), 1
        )
        for g in range(heads):
            query = q_t[part, g]
            s_a = jnp.where(causal, dot(key_a, query, ((1,), (0,))), -FAR)
            s_b = dot(key_b, query, ((1,), (0,)))
            new_top = jnp.maximum(
                jnp.max(s_a, axis=0, keepdims=True), jnp.max(s_b, axis=0, keepdims=True) - pen
            )
            base = new_top * EXP2_SCALE
            p_a = jnp.exp2(s_a * EXP2_SCALE - base).astype(jnp.bfloat16)
            p_b = jnp.exp2(s_b * EXP2_SCALE - (base + pen)).astype(jnp.bfloat16)
            top[slot, g : g + 1, :] = new_top
            acc[slot, g] = dot(vals, jnp.concatenate([p_a, p_b], axis=0), ((1,), (0,)))

    def pair_step(slot, part, number):
        mine = me * 2 + part
        block_a = got_block(0, number)
        block_b = got_block(1, number)
        pen_a = penalty(block_a, mine)
        pen_b = penalty(block_b, mine)
        key_a = keys_of(block_a)
        key_b = keys_of(block_b)
        vals = with_sums(block_a, block_b)
        for g in range(heads):
            query = q_t[part, g]
            s_a = dot(key_a, query, ((1,), (0,)))
            s_b = dot(key_b, query, ((1,), (0,)))
            old_top = top[slot, g : g + 1, :]
            new_top = jnp.maximum(
                old_top,
                jnp.maximum(
                    jnp.max(s_a, axis=0, keepdims=True) - pen_a,
                    jnp.max(s_b, axis=0, keepdims=True) - pen_b,
                ),
            )
            base = new_top * EXP2_SCALE
            p_a = jnp.exp2(s_a * EXP2_SCALE - (base + pen_a)).astype(jnp.bfloat16)
            p_b = jnp.exp2(s_b * EXP2_SCALE - (base + pen_b)).astype(jnp.bfloat16)
            factor = jnp.exp2(old_top * EXP2_SCALE - base)
            top[slot, g : g + 1, :] = new_top
            acc[slot, g] = acc[slot, g] * factor + dot(
                vals, jnp.concatenate([p_a, p_b], axis=0), ((1,), (0,))
            )

    def finish(slot):
        for g in range(heads):
            done = acc[slot, g]
            scaled = done[0:HD] * (1.0 / done[HD : HD + 1])
            att[:, g * HD : (g + 1) * HD] = scaled.T.astype(jnp.bfloat16)

    def core_copy(turn, step):
        cols = pl.ds(step * COLS, COLS)
        return pltpu.make_async_remote_copy(
            src_ref=core_out.at[turn, :, cols],
            dst_ref=core_in.at[turn, :, cols],
            send_sem=core_send.at[turn, step],
            recv_sem=core_recv.at[turn, step],
            device_id=(me, core_peer),
            device_id_type=MESH,
        )

    def y_copy(step):
        cols = pl.ds(step * COLS, COLS)
        return pltpu.make_async_remote_copy(
            src_ref=y_out.at[:, cols],
            dst_ref=y_in.at[:, cols],
            send_sem=y_send.at[step],
            recv_sem=y_recv.at[step],
            device_id=(me, y_peer),
            device_id_type=MESH,
        )

    def project(turn):
        rows = att[...]
        for step in range(steps):
            cols = slice(step * COLS, (step + 1) * COLS)
            sums = dot(rows, w[:, cols], ((1,), (0,)))
            first, second = sums[0:half], sums[half:BLOCK]
            keep_first = core == 0
            own[:, cols] = jnp.where(keep_first, first, second)
            core_out[turn, :, cols] = jnp.where(keep_first, second, first).astype(jnp.bfloat16)
            core_copy(turn, step).start()

    def both_cores(turn, step):
        cols = slice(step * COLS, (step + 1) * COLS)
        core_copy(turn, step).wait_recv()
        return own[:, cols] + core_in[turn, :, cols].astype(jnp.float32), cols

    local_step(0, 1 - y)
    local_step(1, y)

    pages = owner_ref.shape[1]
    slots = table.shape[1]
    mine_col = (owner_ref[...] == me).astype(jnp.int32)
    mine = jnp.broadcast_to(mine_col, (slots, pages)).T[:, 0:1]
    page_row = lax.broadcasted_iota(jnp.int32, (pages, pages), 0)
    page_col = lax.broadcasted_iota(jnp.int32, (pages, pages), 1)
    rank_col = jnp.sum(jnp.where(page_row < page_col, mine, 0), axis=0, keepdims=True)
    slot_col = jnp.where(mine_col > 0, held_ref[me] + rank_col, -1)
    slot_row = jnp.broadcast_to(slot_col, (slots, pages)).T
    slot_number = lax.broadcasted_iota(jnp.int32, (pages, slots), 1)
    page_number = lax.broadcasted_iota(jnp.int32, (pages, slots), 0)
    table[...] = jnp.broadcast_to(
        jnp.sum(jnp.where(slot_row == slot_number, page_number + 1, 0), axis=0, keepdims=True),
        table.shape,
    )
    to_scalars = pltpu.make_async_copy(table, table_s, table_sem)
    to_scalars.start()
    to_scalars.wait()

    @pl.loop(0, n - 1)
    def _(number):
        for lane in range(2):
            hop(lane, number, got_block(lane, number)).wait_recv()

        @pl.when(number < n - 3)
        def _():
            for lane in range(2):
                hop(lane, number + 2, got_block(lane, number)).start()

        pair_step(0, 1 - y, number)

    finish(0)
    loads[3].wait()

    project(0)
    for step in range(steps):
        sums, cols = both_cores(0, step)
        y_out[:, cols] = sums.astype(jnp.bfloat16)
        y_copy(step).start()

    @pl.loop(0, n - 1)
    def _(number):
        pair_step(1, y, number)

    finish(1)

    project(1)

    @pl.loop(0, slots * PAGE // HD, unroll=2)
    def _(group):
        rows = pl.ds(pl.multiple_of(group * HD, HD), HD)
        found = []
        for number in range(HD // PAGE):
            entry = table_s[0, group * (HD // PAGE) + number]
            held = jnp.where(entry > 0, 1.0, 0.0)
            found.append(kv[jnp.maximum(entry - 1, 0)].astype(jnp.float32) * held)
        found = jnp.concatenate(found, axis=0)
        same = lax.broadcasted_iota(jnp.int32, (HD, HD), 0) == lax.broadcasted_iota(
            jnp.int32, (HD, HD), 1
        )
        for t in range(2):
            entries = found[:, t * HD : (t + 1) * HD]
            scale = jnp.max(jnp.abs(entries), axis=1, keepdims=True) + 1e-06
            store_out[rows, t * HD : (t + 1) * HD] = (entries / scale).astype(jnp.bfloat16)
            scale_out[t : t + 1, rows] = jnp.sum(jnp.where(same, scale, 0.0), axis=0, keepdims=True)

    page_copies = [
        pltpu.make_async_copy(store_out, values_hbm, out_sems.at[0]),
        pltpu.make_async_copy(scale_out, scales_hbm, out_sems.at[1]),
    ]
    for copy in page_copies:
        copy.start()

    out_copies = []
    for step in range(steps):
        sums, cols = both_cores(1, step)
        y_copy(step).wait_recv()
        result[:, cols] = (sums + y_in[:, cols].astype(jnp.float32)).astype(jnp.bfloat16)
        span = pl.ds(step * COLS, COLS)
        copy = pltpu.make_async_copy(result.at[:, span], out_hbm.at[:, span], out_sems.at[2 + step])
        copy.start()
        out_copies.append(copy)

    @pl.loop(0, n - 1)
    def _(number):
        for lane in range(2):
            hop(lane, number, block_of(lane, number)).wait_send()

    for step in range(steps):
        core_copy(0, step).wait_send()
        core_copy(1, step).wait_send()
        y_copy(step).wait_send()
    for copy in page_copies + out_copies:
        copy.wait()


def shards(query_states, key_states, value_states, out_weight, block_order, page_owner, held_pages):
    n = lax.axis_size("ctx")
    tok_rows, col_count = query_states.shape
    d_model = out_weight.shape[1]
    heads = col_count // HD
    tokens = n * tok_rows
    pages_dev = tok_rows // PAGE
    slots = 2 * n * max(2, 2 * pages_dev // n)
    steps = d_model // COLS
    part = tok_rows // 4
    bf16, f32 = jnp.bfloat16, jnp.float32
    hbm = pl.BlockSpec(memory_space=pltpu.HBM)
    smem = pl.BlockSpec(memory_space=pltpu.SMEM)
    vmem = pl.BlockSpec(memory_space=pltpu.VMEM)
    layer_output, values, scales = pl.pallas_call(
        functools.partial(kernel, n, heads),
        out_shape=(
            jax.ShapeDtypeStruct((part, d_model), bf16),
            jax.ShapeDtypeStruct((slots * PAGE, 2 * HD), bf16),
            jax.ShapeDtypeStruct((2, slots * PAGE), f32),
        ),
        in_specs=[hbm] * 4 + [smem, vmem, smem],
        out_specs=(hbm,) * 3,
        scratch_shapes=[
            pltpu.VMEM((tokens // PAGE, PAGE, 2 * HD), bf16),
            pltpu.VMEM((tok_rows, col_count), bf16),
            pltpu.VMEM((2, heads, HD, BLOCK), bf16),
            pltpu.VMEM(out_weight.shape, bf16),
            pltpu.VMEM((2, 8, BLOCK), f32),
            pltpu.VMEM((2, heads, HD + SUM_ROWS, BLOCK), f32),
            pltpu.VMEM((BLOCK, col_count), bf16),
            pltpu.VMEM((part, d_model), f32),
            pltpu.VMEM((2, part, d_model), bf16),
            pltpu.VMEM((2, part, d_model), bf16),
            pltpu.VMEM((part, d_model), bf16),
            pltpu.VMEM((part, d_model), bf16),
            pltpu.VMEM((part, d_model), bf16),
            pltpu.VMEM((8, slots), jnp.int32),
            pltpu.SMEM((8, slots), jnp.int32),
            pltpu.VMEM((slots * PAGE, 2 * HD), bf16),
            pltpu.VMEM((2, slots * PAGE), f32),
            pltpu.SemaphoreType.DMA((4,)),
            pltpu.SemaphoreType.DMA((2, n - 1)),
            pltpu.SemaphoreType.DMA((2, n - 1)),
            pltpu.SemaphoreType.DMA((2, steps)),
            pltpu.SemaphoreType.DMA((2, steps)),
            pltpu.SemaphoreType.DMA((steps,)),
            pltpu.SemaphoreType.DMA((steps,)),
            pltpu.SemaphoreType.DMA,
            pltpu.SemaphoreType.DMA((2 + steps,)),
        ],
        compiler_params=pltpu.CompilerParams(
            collective_id=0, has_side_effects=True, vmem_limit_bytes=63 * 1024 * 1024
        ),
    )(
        query_states,
        key_states.reshape(-1, PAGE, HD),
        value_states.reshape(-1, PAGE, HD),
        out_weight,
        block_order,
        page_owner.reshape(1, -1),
        held_pages,
    )
    return layer_output, values.reshape(slots, PAGE, 2 * HD), scales


def solution(mesh):
    in_specs = (
        P("ctx", "head"),
        P("ctx", "head"),
        P("ctx", "head"),
        P("head", None),
        P(),
        P(),
        P(),
    )
    out_specs = (P(("ctx", "head"), None), P("ctx", None, "head"), P("head", "ctx"))
    return jax.shard_map(shards, mesh=mesh, in_specs=in_specs, out_specs=out_specs, check_vma=False)
```
